512 devices in a mesh: dp: 32 (over y, z_lo), tensor: 16 (over x, z_hi, core).
Axes of the slice: x: 4, y: 8, z: 8 (z_hi: 2, z_lo: 4; z = z_hi * 4 + z_lo), core: 2. Of those that a mesh axis runs over, the one named last changes fastest.
Arguments:
- tokens: bfloat16 [4096, 16384], P('dp', 'tensor'), may hold values from -6 to 6
- query_key_value_weight: bfloat16 [16384, 12288], P('tensor', 'dp'), may hold values from -0.046875 to 0.046875
- adapter_down_weight: bfloat16 [32, 16, 16384], P(None, None, 'tensor'), may hold values from -0.046875 to 0.046875
- adapter_up_weight: bfloat16 [32, 16, 12288], P(None, None, 'dp'), may hold values from -1.5 to 1.5
- adapter_per_block: int32 [32], replicated, may hold values from 0 to 31
Outputs:
- projected: bfloat16 [4096, 12288], P('tensor', 'dp')
The draws below stay inside these ranges and needn't reach their ends.
All inputs are finite; a program needn't handle non-finite values.
Results may differ from the reference program's by a relative error of at most 0.02.
Values may be sent and summed in bfloat16 or wider, within the bound.
No kernel may reach another device: no remote copies, remote signals or barrier semaphores. Data moves between devices by JAX's collectives and lax.ppermute only.
A program may use at most 64 MiB of HBM per device.

```python
import jax
import jax.numpy as jnp

MODEL_WIDTH = 16384
ADAPTER_RANK = 16
ADAPTER_COUNT = 32
BLOCK = 128
FEATURE_COLUMNS = 12288
TOKENS = 4096
BLOCKS = 32
N_TENSOR = 16


def plant(values, own_key, low, top_value):
    longest = values.shape.index(max(values.shape))
    spots = []
    for shift in (0, 1):
        where = [jax.random.randint(jax.random.fold_in(own_key, axis), (), 0, length) for axis, length in enumerate(values.shape)]
        where[longest] = (where[longest] + shift) % values.shape[longest]
        spots.append(tuple(where))
    return values.at[spots[0]].set(low).at[spots[1]].set(top_value)


def block_scale(rng, shape, split, least, top_value):
    loudness, own = 1.0, jax.random.fold_in(rng, 6)
    for position, parts in split:
        heights = jnp.exp(jax.random.uniform(jax.random.fold_in(own, position), (parts,), jnp.float32, least / len(split), top_value / len(split)))
        loudness = loudness * jnp.repeat(heights, shape[position] // parts).reshape([-1 if axis == position else 1 for axis in range(len(shape))])
    return loudness


def scatter_about(own_key, extent, deviation, bound, cuts=(), kind=jnp.bfloat16):
    result = deviation * jax.random.normal(own_key, extent, jnp.float32)
    if cuts:
        result = result * block_scale(own_key, extent, cuts, -0.22, 0.18)
    return jnp.clip(result, -bound, bound).astype(kind)


def setup_inputs(seed: int = 0) -> dict:
    key_list = jax.random.split(jax.random.key(seed), 6)
    return {
        "tokens": scatter_about(key_list[0], (TOKENS, MODEL_WIDTH), 1.0, 6.0, ((0, 32), (1, 16))),
        "query_key_value_weight": scatter_about(key_list[1], (MODEL_WIDTH, FEATURE_COLUMNS), MODEL_WIDTH ** -0.5, 0.046875, ((0, 16), (1, 32))),
        "adapter_down_weight": scatter_about(key_list[2], (ADAPTER_COUNT, ADAPTER_RANK, MODEL_WIDTH), MODEL_WIDTH ** -0.5, 0.046875, ((2, 16),)),
        "adapter_up_weight": scatter_about(key_list[3], (ADAPTER_COUNT, ADAPTER_RANK, FEATURE_COLUMNS), ADAPTER_RANK ** -0.5, 1.5, ((2, 32),)),
        "adapter_per_block": plant(jax.random.randint(key_list[4], (BLOCKS,), 0, ADAPTER_COUNT), jax.random.fold_in(key_list[4], 1), 0, ADAPTER_COUNT - 1).astype(jnp.int32),
    }


def reference(tokens, query_key_value_weight, adapter_down_weight, adapter_up_weight, adapter_per_block):
    part = MODEL_WIDTH // N_TENSOR
    blocks = TOKENS // BLOCK
    down_weights = adapter_down_weight[adapter_per_block]
    up_weights = adapter_up_weight[adapter_per_block]
    base = jnp.zeros((TOKENS, FEATURE_COLUMNS), jnp.float32)
    shrink_total = jnp.zeros((blocks, BLOCK, ADAPTER_RANK), jnp.float32)
    for index in range(N_TENSOR):
        tok_part = tokens[:, index * part:(index + 1) * part]
        term = jnp.dot(tok_part, query_key_value_weight[index * part:(index + 1) * part], preferred_element_type=jnp.float32)
        base = base + term.astype(jnp.bfloat16).astype(jnp.float32)
        tok_blocks = tok_part.reshape(blocks, BLOCK, part).astype(jnp.float32)
        down_part = down_weights[:, :, index * part:(index + 1) * part].astype(jnp.float32)
        shrink_term = jnp.einsum("btd,brd->btr", tok_blocks, down_part)
        shrink_total = shrink_total + shrink_term.astype(jnp.bfloat16).astype(jnp.float32)
    shrink = shrink_total.astype(jnp.bfloat16).astype(jnp.float32)
    expand = jnp.einsum("btr,brf->btf", shrink, up_weights.astype(jnp.float32)).reshape(TOKENS, FEATURE_COLUMNS)
    return (base + 0.5 * expand).astype(jnp.bfloat16)
```

```python
import jax
import jax.numpy as jnp
from jax import lax
from jax.experimental import pallas as pl
from jax.experimental.pallas import tpu as pltpu
from jax.sharding import Mesh, PartitionSpec as P

BLOCK = 128
Y, ZP, ZQ, X, ZH, C = 8, 2, 2, 4, 2, 2
AXES = ("y", "p", "q", "x", "zh", "c")
DP, TENSOR = ("y", "p", "q"), ("x", "zh", "c")


def ring(axis, size, step):
    return [(i, (i + step) % size) for i in range(size)]


def project(order, tokens, down, keep_w, send_w, keep, send):
    rows, features = tokens.shape
    rank = down.shape[0] // 2
    tile = pl.program_id(0)
    tok = tokens[...]
    shrink = lax.dot_general(
        tok, down[...], (((1,), (1,)), ((), ())), preferred_element_type=jnp.float32
    )
    row = lax.broadcasted_iota(jnp.int32, shrink.shape, 0) // BLOCK
    col = lax.broadcasted_iota(jnp.int32, shrink.shape, 1) // rank
    low = jnp.where(row == col, 0.5 * shrink, 0.0).astype(jnp.bfloat16)
    ups = pl.ds(pl.multiple_of(features + tile * 2 * rank, 2 * rank), 2 * rank)
    for w, out in ((keep_w, keep), (send_w, send)):
        total = jnp.dot(tok, w[:features, :], preferred_element_type=jnp.float32)
        total += jnp.dot(low, w[ups, :], preferred_element_type=jnp.float32)
        out[...] = total.astype(out.dtype)


def partials(x, gathered, down, keep_w, send_w):
    tiles, rows, features = gathered.shape
    columns = keep_w.shape[1]

    def place(t, order):
        return ((t // 2 - order[0] + X) % X * 2 + t % 2, 0, 0)

    whole = pl.BlockSpec(keep_w.shape, lambda t, order: (0, 0))
    out = jax.ShapeDtypeStruct((tiles, rows, columns), jnp.bfloat16)
    return pl.pallas_call(
        project,
        out_shape=(out, out),
        grid_spec=pltpu.PrefetchScalarGridSpec(
            num_scalar_prefetch=1,
            grid=(tiles,),
            in_specs=[
                pl.BlockSpec((None, rows, features), lambda t, order: (t, 0, 0)),
                pl.BlockSpec((None,) + down.shape[1:], lambda t, order: (t, 0, 0)),
                whole,
                whole,
            ],
            out_specs=[pl.BlockSpec((None, rows, columns), place)] * 2,
        ),
        compiler_params=pltpu.CompilerParams(vmem_limit_bytes=32 * 1024 * 1024),
        cost_estimate=pl.CostEstimate(
            flops=4 * tiles * rows * features * columns,
            bytes_accessed=2 * (gathered.size + 2 * tiles * rows * columns),
            transcendentals=0,
        ),
    )(x.reshape(1), gathered, down, keep_w, send_w)


def local(
    tokens, query_key_value_weight, adapter_down_weight, adapter_up_weight, adapter_per_block
):
    p, q, x, zh, c = (lax.axis_index(a) for a in AXES[1:])
    own_rows, features = tokens.shape
    columns = query_key_value_weight.shape[1]
    rank = adapter_down_weight.shape[1]

    other = lax.ppermute(tokens, "q", ring("q", ZQ, 1))
    gathered = lax.all_gather(jnp.concatenate([tokens, other], 0), "y", axis=0, tiled=False)

    per = adapter_per_block.reshape(Y, ZP, ZQ)
    per = jnp.where(q == 0, per, per[:, :, ::-1])
    mine = jnp.where(p == 0, per[:, 0], per[:, 1])
    theirs = jnp.where(p == 0, per[:, 1], per[:, 0])
    down = adapter_down_weight[mine.reshape(-1)].reshape(Y, ZQ * rank, features)
    up_mine = adapter_up_weight[mine.reshape(-1)].reshape(-1, columns)
    up_theirs = adapter_up_weight[theirs.reshape(-1)].reshape(-1, columns)

    own_w = jnp.concatenate([query_key_value_weight, up_mine], 0)
    their_w = lax.ppermute(
        jnp.concatenate([query_key_value_weight, up_theirs], 0), "p", ring("p", ZP, 1)
    )
    keep_w = jnp.where(c == p, own_w, their_w)
    send_w = jnp.where(c == p, their_w, own_w)

    keep, send = partials(x, gathered, down, keep_w, send_w)
    received = lax.ppermute(send, "c", ring("c", C, 1))

    def added(d):
        a, b = keep[2 * d : 2 * d + 2], received[2 * d : 2 * d + 2]
        return a.astype(jnp.float32) + b.astype(jnp.float32)

    total = added(0)
    for d in (2, 1, 3):
        total += lax.ppermute(added(d).astype(jnp.bfloat16), "x", ring("x", X, d)).astype(
            jnp.float32
        )
    total = total.astype(jnp.bfloat16)

    here = jnp.where(zh == 0, total[0], total[1])
    there = jnp.where(zh == 0, total[1], total[0])
    swap = [(i * 4 + h * 2 + j, j * 4 + h * 2 + i) for i in range(ZP) for h in range(ZH) for j in range(C)]
    cross = [(i * 4 + h * 2 + j, j * 4 + (1 - h) * 2 + i) for i in range(ZP) for h in range(ZH) for j in range(C)]
    far = lax.ppermute(there, ("p", "zh", "c"), cross)
    near = lax.ppermute(here, ("p", "zh", "c"), swap)
    out = near.astype(jnp.float32) + far.astype(jnp.float32)
    out = out.reshape(ZQ, own_rows, columns)
    out = jnp.where(q == 0, out, out[::-1])
    return out.reshape(ZQ * own_rows, columns).astype(jnp.bfloat16)


def solution(mesh):
    physical = Mesh(mesh.devices.reshape(Y, ZP, ZQ, X, ZH, C), AXES)
    return jax.shard_map(
        local,
        mesh=physical,
        in_specs=(
            P(DP, TENSOR),
            P(TENSOR, DP),
            P(None, None, TENSOR),
            P(None, None, DP),
            P(),
        ),
        out_specs=P(TENSOR, DP),
        check_vma=False,
    )
```

```python
import jax
import jax.numpy as jnp
from jax import lax
from jax.experimental import pallas as pl
from jax.experimental.pallas import tpu as pltpu
from jax.sharding import Mesh, PartitionSpec as P

BLOCK = 128
HALF = BLOCK // 2
Y, ZP, ZQ, X, ZH, C = 8, 2, 2, 4, 2, 2
AXES = ("y", "p", "q", "x", "zh", "c")
DP, TENSOR = ("y", "p", "q"), ("x", "zh", "c")
VMEM_BYTES = 56 * 1024 * 1024


def flip(size):
    return [(i, i ^ 1) for i in range(size)]


def stack_rows(half, tokens, along_q, along_x, along_qx, out):
    out[:HALF] = tokens[pl.ds(pl.multiple_of(half[0] * HALF, HALF), HALF), :]
    out[HALF : 2 * HALF] = along_q[...]
    out[2 * HALF : 3 * HALF] = along_x[...]
    out[3 * HALF :] = along_qx[...]


def stacked(half, tokens, *received):
    whole = pl.BlockSpec(memory_space=pltpu.VMEM)
    return pl.pallas_call(
        stack_rows,
        out_shape=jax.ShapeDtypeStruct((4 * HALF, tokens.shape[1]), tokens.dtype),
        in_specs=[pl.BlockSpec(memory_space=pltpu.SMEM)] + [whole] * 4,
        out_specs=whole,
    )(half.reshape(1), tokens, *received)


def project(order, tokens, down, weight, up, keep, send):
    tiles, rows, features = tokens.shape
    columns = keep.shape[1]
    rank = down.shape[1] // (tiles * ZQ)
    mine = tokens[:, : rows // 2, :].reshape(-1, features)
    pair = tokens[:, rows // 2 :, :].reshape(-1, features)
    across = (((1,), (1,)), ((), ()))
    shrink = lax.dot_general(mine, down[0], across, preferred_element_type=jnp.float32)
    shrink += lax.dot_general(pair, down[1], across, preferred_element_type=jnp.float32)
    row = lax.broadcasted_iota(jnp.int32, shrink.shape, 0) // HALF
    col = lax.broadcasted_iota(jnp.int32, shrink.shape, 1) // rank
    low = jnp.where(row == col, 0.5 * shrink, 0.0).astype(jnp.bfloat16)
    total = jnp.dot(mine, weight[0], preferred_element_type=jnp.float32)
    total += jnp.dot(pair, weight[1], preferred_element_type=jnp.float32)
    total += jnp.dot(low, up[...], preferred_element_type=jnp.float32)
    total = total.astype(keep.dtype)
    keep[...] = total[:, :columns]
    send[...] = total[:, columns:]


def partials(x, gathered, down, weight, up):
    rows, features = gathered.shape[1:]
    columns = weight.shape[2] // 2

    def place(t, order):
        return (t + order[0]) % X

    out = jax.ShapeDtypeStruct((X, rows, columns), jnp.bfloat16)
    return pl.pallas_call(
        project,
        out_shape=(out, out),
        grid_spec=pltpu.PrefetchScalarGridSpec(
            num_scalar_prefetch=1,
            grid=(X,),
            in_specs=[
                pl.BlockSpec((2, rows, features), lambda t, order: (place(t, order), 0, 0)),
                pl.BlockSpec(
                    (2, None) + down.shape[2:], lambda t, order: (0, place(t, order), 0, 0)
                ),
                pl.BlockSpec(weight.shape, lambda t, order: (0, 0, 0)),
                pl.BlockSpec((None,) + up.shape[1:], lambda t, order: (place(t, order), 0, 0)),
            ],
            out_specs=[pl.BlockSpec((None, rows, columns), lambda t, order: (t, 0, 0))] * 2,
        ),
        compiler_params=pltpu.CompilerParams(vmem_limit_bytes=VMEM_BYTES),
        cost_estimate=pl.CostEstimate(
            flops=4 * gathered.size * columns,
            bytes_accessed=2 * (gathered.size + weight.size + 2 * X * rows * columns),
            transcendentals=0,
        ),
    )(x.reshape(1), gathered, down, weight, up)


def local(
    tokens, query_key_value_weight, adapter_down_weight, adapter_up_weight, adapter_per_block
):
    p, q, x, zh, c = (lax.axis_index(a) for a in AXES[1:])
    features = tokens.shape[1]
    columns = query_key_value_weight.shape[1]
    rank = adapter_down_weight.shape[1]
    half = x % 2

    same = lax.dynamic_slice_in_dim(tokens, half * HALF, HALF, 0)
    rest = lax.dynamic_slice_in_dim(tokens, (1 - half) * HALF, HALF, 0)
    along_q = lax.ppermute(same, "q", flip(ZQ))
    along_x = lax.ppermute(rest, "x", flip(X))
    along_qx = lax.ppermute(
        rest, ("q", "x"), [(i * X + j, (1 - i) * X + (j ^ 1)) for i in range(ZQ) for j in range(X)]
    )
    rows = stacked(half, tokens, along_q, along_x, along_qx)
    gathered = lax.all_gather(rows, "y", axis=0, tiled=False)

    first = query_key_value_weight
    second = lax.ppermute(first, "p", flip(ZP))
    first_pair = lax.ppermute(first, "x", flip(X))
    second_pair = lax.ppermute(second, "x", flip(X))
    mine_kept = c == p
    weight = jnp.stack(
        [
            jnp.where(mine_kept, jnp.concatenate(v, 1), jnp.concatenate(v[::-1], 1))
            for v in ((first, second), (first_pair, second_pair))
        ]
    )

    per = adapter_per_block.reshape(Y, ZP, ZQ)
    per = jnp.where(q == 0, per, per[:, :, ::-1])
    mine = jnp.where(p == 0, per[:, 0], per[:, 1]).reshape(-1)
    theirs = jnp.where(p == 0, per[:, 1], per[:, 0]).reshape(-1)
    down = adapter_down_weight[mine].reshape(X, 2 * ZQ * rank, features)
    down = jnp.stack([down, lax.ppermute(down, "x", flip(X))])
    up_first = adapter_up_weight[mine].reshape(X, 2 * ZQ * rank, columns)
    up_second = lax.ppermute(
        adapter_up_weight[theirs].reshape(X, 2 * ZQ * rank, columns), "p", flip(ZP)
    )
    up = jnp.where(
        mine_kept,
        jnp.concatenate([up_first, up_second], 2),
        jnp.concatenate([up_second, up_first], 2),
    )

    keep, send = partials(x, gathered, down, weight, up)
    received = lax.ppermute(send, "c", flip(C))

    def added(d):
        return keep[d].astype(jnp.float32) + received[d].astype(jnp.float32)

    def moved(d):
        shift = [(i, (i + d) % X) for i in range(X)]
        return lax.ppermute(added(d).astype(jnp.bfloat16), "x", shift).astype(jnp.float32)

    across = moved(2)
    beside = moved(1) + moved(3)
    total = jnp.stack([added(0) + across, beside]).astype(jnp.bfloat16)
    total = total.reshape(2, ZH, ZQ * HALF, columns)

    here = jnp.where(zh == 0, total[:, 0], total[:, 1])
    there = jnp.where(zh == 0, total[:, 1], total[:, 0])
    places = [(i, h, j) for i in range(ZP) for h in range(ZH) for j in range(C)]
    swap = [(i * 4 + h * 2 + j, j * 4 + h * 2 + i) for i, h, j in places]
    cross = [(i * 4 + h * 2 + j, j * 4 + (1 - h) * 2 + i) for i, h, j in places]
    far = lax.ppermute(there, ("p", "zh", "c"), cross)
    near = lax.ppermute(here, ("p", "zh", "c"), swap)
    out = near.astype(jnp.float32) + far.astype(jnp.float32)
    out = out.reshape(2, ZQ, HALF, columns)
    out = jnp.where(half == 0, out, out[::-1])
    out = jnp.where(q == 0, out, out[:, ::-1])
    return out.transpose(1, 0, 2, 3).reshape(ZQ * BLOCK, columns).astype(jnp.bfloat16)


def solution(mesh):
    physical = Mesh(mesh.devices.reshape(Y, ZP, ZQ, X, ZH, C), AXES)
    return jax.shard_map(
        local,
        mesh=physical,
        in_specs=(
            P(DP, TENSOR),
            P(TENSOR, DP),
            P(None, None, TENSOR),
            P(None, None, DP),
            P(),
        ),
        out_specs=P(TENSOR, DP),
        check_vma=False,
    )
```

```python
import jax
import jax.numpy as jnp
from jax import lax
from jax.experimental import pallas as pl
from jax.experimental.pallas import tpu as pltpu
from jax.sharding import Mesh, PartitionSpec as P

Y, ZP, ZQ, X, ZH, C = 8, 2, 2, 4, 2, 2
AXES = ("y", "p", "q", "x", "zh", "c")
DP, TENSOR = ("y", "p", "q"), ("x", "zh", "c")
VMEM_BYTES = 48_000_000
SMALL_VMEM_BYTES = 16_000_000
DOWN_COLUMNS = 512


def flip(size):
    return [(i, i ^ 1) for i in range(size)]


def copied(moves):
    for move in moves:
        move.start()
    for move in moves:
        move.wait()


def join_features(first, second, out, sems):
    width = first.shape[1]
    copied(
        [
            pltpu.make_async_copy(v, out.at[:, pl.ds(i * width, width)], sems.at[i])
            for i, v in enumerate((first, second))
        ]
    )


def joined(first, second):
    rows, width = first.shape
    return pl.pallas_call(
        join_features,
        out_shape=jax.ShapeDtypeStruct((rows, 2 * width), first.dtype),
        in_specs=[pl.BlockSpec(memory_space=pltpu.VMEM)] * 2,
        out_specs=pl.BlockSpec(memory_space=pl.ANY),
        scratch_shapes=[pltpu.SemaphoreType.DMA((2,))],
        compiler_params=pltpu.CompilerParams(vmem_limit_bytes=SMALL_VMEM_BYTES),
    )(first, second)


def place_weights(slots, *refs):
    ins, (table, sems) = refs[:-2], refs[-2:]
    first, *halves = ins[:3]
    pair, *pair_halves = ins[3:6]
    up, up_swapped, down_own, down_pair = ins[6:]
    features, columns = first.shape
    moves = []

    def move(source, row, col):
        at = tuple(
            pl.ds(pl.multiple_of(i, 128), n) for i, n in zip((row, col), source.shape)
        )
        moves.append(pltpu.make_async_copy(source, table.at[at], sems.at[len(moves)]))

    own, other = slots[1] * columns, (1 - slots[1]) * columns
    for k, whole, split in ((slots[0], first, halves), (1 - slots[0], pair, pair_halves)):
        move(whole, k * features, own)
        for i, v in enumerate(split):
            move(v, k * features + i * v.shape[0], other)
    move(up, 2 * features, own)
    move(up_swapped, 2 * features, other)
    ranks = down_own.shape[0]
    for k, v in ((slots[0], down_own), (1 - slots[0], down_pair)):
        for i in range(features // DOWN_COLUMNS):
            row = 2 * features + ranks * (1 + k * (features // DOWN_COLUMNS) + i)
            move(v.at[:, pl.ds(i * DOWN_COLUMNS, DOWN_COLUMNS)], row, 0)
    copied(moves)


def placed(slots, parts):
    features, columns = parts[0].shape
    ranks = parts[-1].shape[0]
    down_rows = 2 * features // DOWN_COLUMNS * ranks
    return pl.pallas_call(
        place_weights,
        out_shape=pltpu.VMEM((2 * features + ranks + down_rows, 2 * columns), parts[0].dtype),
        in_specs=[pl.BlockSpec(memory_space=pltpu.SMEM)]
        + [pl.BlockSpec(memory_space=pl.ANY)] * len(parts),
        out_specs=pl.BlockSpec(memory_space=pltpu.VMEM),
        scratch_shapes=[pltpu.SemaphoreType.DMA((16,))],
        compiler_params=pltpu.CompilerParams(vmem_limit_bytes=SMALL_VMEM_BYTES),
    )(slots, *parts)


def project(order, tokens, table, keep, send, held, sems):
    step = pl.program_id(0)
    rows, features = tokens.shape[1:]
    ranks = held.shape[3] - features
    rank = ranks // Y
    tiles, tile_rows, columns = keep.shape
    groups = tile_rows // rows

    def fetch(t):
        at = pl.ds((t + order[0]) % X * groups, groups)
        return pltpu.make_async_copy(
            tokens.at[at], held.at[t, :, :, pl.ds(0, features)], sems.at[t]
        )

    @pl.when(step == 0)
    def _():
        for t in range(X):
            fetch(t).start()

    here = [step * tiles + i for i in range(tiles)]
    for t in here:
        fetch(t).wait()
    for t in here:
        shrink = 0.0
        for i in range(features // DOWN_COLUMNS):
            at = slice(i * DOWN_COLUMNS, (i + 1) * DOWN_COLUMNS)
            start = features + (1 + i) * ranks
            shrink += lax.dot_general(
                held[t, :, :, at].reshape(tile_rows, DOWN_COLUMNS),
                table[start : start + ranks, :DOWN_COLUMNS],
                (((1,), (1,)), ((), ())),
                preferred_element_type=jnp.float32,
            )
        block = lax.broadcasted_iota(jnp.int32, shrink.shape, 0) // rows
        block += (t + order[0]) % X * groups
        adapter = lax.broadcasted_iota(jnp.int32, shrink.shape, 1) // rank
        low = jnp.where(block == adapter, 0.5 * shrink, 0.0).astype(held.dtype)
        held[t, :, :, features:] = low.reshape(groups, rows, ranks)
    for i, t in enumerate(here):
        tok = held[t].reshape(tile_rows, features + ranks)
        total = jnp.dot(tok, table[: features + ranks], preferred_element_type=jnp.float32)
        total = total.astype(keep.dtype)
        keep[i] = total[:, :columns]
        send[i] = total[:, columns:]


def partials(x, gathered, table, ranks):
    rows, features = gathered.shape[1:]
    columns = table.shape[1] // 2
    groups = Y // X
    tiles = 2
    out = jax.ShapeDtypeStruct((X, groups * rows, columns), jnp.bfloat16)
    return pl.pallas_call(
        project,
        out_shape=(out, out),
        grid_spec=pltpu.PrefetchScalarGridSpec(
            num_scalar_prefetch=1,
            grid=(X // tiles,),
            in_specs=[
                pl.BlockSpec(memory_space=pltpu.HBM),
                pl.BlockSpec(memory_space=pltpu.VMEM),
            ],
            out_specs=[
                pl.BlockSpec((tiles,) + out.shape[1:], lambda t, order: (t, 0, 0))
            ]
            * 2,
            scratch_shapes=[
                pltpu.VMEM((X, groups, rows, features + ranks), jnp.bfloat16),
                pltpu.SemaphoreType.DMA((X,)),
            ],
        ),
        compiler_params=pltpu.CompilerParams(vmem_limit_bytes=VMEM_BYTES),
        cost_estimate=pl.CostEstimate(
            flops=4 * gathered.size * columns,
            bytes_accessed=2 * (gathered.size + table.size + 2 * out.size),
            transcendentals=0,
        ),
    )(x.reshape(1), gathered, table)


def local(
    tokens, query_key_value_weight, adapter_down_weight, adapter_up_weight, adapter_per_block
):
    p, q, x, zh, c = (lax.axis_index(a) for a in AXES[1:])
    rows, features = tokens.shape
    columns = query_key_value_weight.shape[1]
    half = x % 2
    order = jnp.where(q == half, 0, 1)

    grid = [(i, j) for i in range(ZQ) for j in range(X)]

    def over(target):
        return [(i * X + j, target(i, j)) for i, j in grid]

    first = lax.ppermute(
        tokens, ("q", "x"), over(lambda i, j: i * X + j if i == j % 2 else (1 - i) * X + (j ^ 1))
    )
    second = lax.ppermute(
        tokens, ("q", "x"), over(lambda i, j: (1 - i) * X + j if i == j % 2 else i * X + (j ^ 1))
    )
    gathered = lax.all_gather(joined(first, second), "y", axis=0, tiled=False)

    per = adapter_per_block.reshape(Y, ZP, ZQ)

    def adapters(i, j):
        return lax.dynamic_slice(per, (0, i, j), (Y, 1, 1)).reshape(Y)

    def taken(table, i, j):
        return table[adapters(i, j)].reshape(-1, table.shape[2])

    down = taken(adapter_down_weight, p, half)
    down_pair = lax.ppermute(taken(adapter_down_weight, p, 1 - half), "x", flip(X))
    up = taken(adapter_up_weight, p, half)
    up_swapped = lax.ppermute(taken(adapter_up_weight, 1 - p, half), "p", flip(ZP))

    own = query_key_value_weight
    pair = lax.ppermute(own, "x", flip(X))
    swapped = [lax.ppermute(v, "p", flip(ZP)) for v in jnp.split(own, 2)]
    swapped_pair = [lax.ppermute(v, "x", flip(X)) for v in swapped]
    slots = jnp.stack([order, jnp.where(c == p, 0, 1)]).astype(jnp.int32)
    table = placed(
        slots, [own, *swapped, pair, *swapped_pair, up, up_swapped, down, down_pair]
    )

    keep, send = partials(x, gathered, table, down.shape[0])
    received = lax.ppermute(send, "c", flip(C))

    def added(d):
        return keep[d].astype(jnp.float32) + received[d].astype(jnp.float32)

    def moved(d):
        shift = [(i, (i + d) % X) for i in range(X)]
        return lax.ppermute(added(d).astype(jnp.bfloat16), "x", shift).astype(jnp.float32)

    across = moved(2)
    beside = moved(3) + moved(1)
    total = jnp.stack([added(0) + across, beside]).astype(jnp.bfloat16)
    total = total.reshape(2, ZH, rows, columns)

    here = jnp.where(zh == 0, total[:, 0], total[:, 1])
    there = jnp.where(zh == 0, total[:, 1], total[:, 0])
    places = [(i, h, j) for i in range(ZP) for h in range(ZH) for j in range(C)]
    swap = [(i * 4 + h * 2 + j, j * 4 + h * 2 + i) for i, h, j in places]
    cross = [(i * 4 + h * 2 + j, j * 4 + (1 - h) * 2 + i) for i, h, j in places]
    far = lax.ppermute(there, ("p", "zh", "c"), cross)
    near = lax.ppermute(here, ("p", "zh", "c"), swap)
    out = near.astype(jnp.float32) + far.astype(jnp.float32)
    out = jnp.where(half == 0, out, out[::-1])
    return out.reshape(ZQ * rows, columns).astype(jnp.bfloat16)


def solution(mesh):
    physical = Mesh(mesh.devices.reshape(Y, ZP, ZQ, X, ZH, C), AXES)
    return jax.shard_map(
        local,
        mesh=physical,
        in_specs=(
            P(DP, TENSOR),
            P(TENSOR, DP),
            P(None, None, TENSOR),
            P(None, None, DP),
            P(),
        ),
        out_specs=P(TENSOR, DP),
        check_vma=False,
    )
```

```python
import functools

import jax
import jax.numpy as jnp
from jax import lax
from jax.experimental import pallas as pl
from jax.experimental.pallas import tpu as pltpu
from jax.sharding import Mesh, PartitionSpec as P

Y, ZP, ZQ, X, ZH, C = 8, 2, 2, 4, 2, 2
AXES = ("y", "p", "q", "x", "zh", "c")
DP, TENSOR = ("y", "p", "q"), ("x", "zh", "c")
GROUPS = Y // X
VMEM_BYTES = 16_000_000
PLACE_FLOPS = 10_000_000_000
OFFSETS = (0, -1, 1, -2, 2, -3, 3, 4)
VMEM = pl.BlockSpec(memory_space=pltpu.VMEM)
SMEM = pl.BlockSpec(memory_space=pltpu.SMEM)
ANY = pl.BlockSpec(memory_space=pl.ANY)
PARAMS = pltpu.CompilerParams(vmem_limit_bytes=VMEM_BYTES)


def flip(size):
    return [(i, i ^ 1) for i in range(size)]


def copied(moves):
    for move in moves:
        move.start()
    for move in moves:
        move.wait()


def block_of(where, i, p):
    return (i // ZQ) * ZP * ZQ + p * ZQ + (where[2] ^ (i % ZQ))


def join_rows(first, second, out):
    rows = first.shape[0]
    out[:rows] = first[...]
    out[rows:] = second[...]


def joined(first, second):
    rows, features = first.shape
    return pl.pallas_call(
        join_rows,
        out_shape=jax.ShapeDtypeStruct((2 * rows, features), first.dtype),
        in_specs=[VMEM] * 2,
        out_specs=VMEM,
        compiler_params=PARAMS,
    )(first, second)


def pick_up_rows(where, adapter, up, out, sems):
    rank = up.shape[1]
    copied(
        [
            pltpu.make_async_copy(
                up.at[adapter[block_of(where, i, 1 - where[1])]],
                out.at[pl.ds(i * rank, rank)],
                sems.at[i],
            )
            for i in range(Y * ZQ)
        ]
    )


def picked(where, adapter, up):
    rank, columns = up.shape[1:]
    return pl.pallas_call(
        pick_up_rows,
        out_shape=jax.ShapeDtypeStruct((Y * ZQ * rank, columns), up.dtype),
        in_specs=[SMEM, SMEM, ANY],
        out_specs=VMEM,
        scratch_shapes=[pltpu.SemaphoreType.DMA((Y * ZQ,))],
        compiler_params=PARAMS,
    )(where, adapter, up)


def place_table(where, adapter, down, up, first, *refs):
    swapped, (table, downs, sems) = refs[:-3], refs[-3:]
    features, columns = first.shape
    rank = up.shape[1]
    moves = []

    def move(source, target):
        moves.append(pltpu.make_async_copy(source, target, sems.at[len(moves)]))

    def part(row, rows, col):
        cols = pl.ds(pl.multiple_of(col * columns, 128), columns)
        return table.at[pl.ds(row, rows), cols]

    own, other = where[4], 1 - where[4]
    move(first, part(0, features, own))
    row = 0
    for v in swapped:
        move(v, part(row, v.shape[0], other))
        row += v.shape[0]
    for i in range(Y * ZQ):
        index = adapter[block_of(where, i, where[1])]
        move(up.at[index], part(features + i * rank, rank, own))
        move(down.at[index], downs.at[pl.ds(i * rank, rank)])
    copied(moves)


def placed(where, adapter, down, up, first, swapped):
    features, columns = first.shape
    ranks = Y * ZQ * up.shape[1]
    return pl.pallas_call(
        place_table,
        out_shape=(
            jax.ShapeDtypeStruct((features + ranks, 2 * columns), first.dtype),
            jax.ShapeDtypeStruct((ranks, features), first.dtype),
        ),
        in_specs=[SMEM] * 2 + [ANY] * (3 + len(swapped)),
        out_specs=(VMEM, VMEM),
        scratch_shapes=[pltpu.SemaphoreType.DMA((1 + len(swapped) + 2 * Y * ZQ,))],
        compiler_params=PARAMS,
        cost_estimate=pl.CostEstimate(
            flops=PLACE_FLOPS, bytes_accessed=4 * first.size, transcendentals=0
        ),
    )(where, adapter, down, up, first, *swapped)


def project(offsets, where, table, downs, *refs):
    count = len(offsets)
    chunks, (keep, send, held, made, fetches, stores) = refs[:count], refs[-6:]
    rows, features = chunks[0].shape
    ranks = downs.shape[0]
    columns = table.shape[1] // 2
    y, x = where[0], where[3]
    sources = [(y + offset + Y) % Y for offset in offsets]

    def fetch(i):
        at = held.at[i, :, pl.ds(0, features)]
        return pltpu.make_async_copy(chunks[i], at, fetches.at[i])

    def store(i, j, out):
        tile, group = (sources[i] // GROUPS - x + X) % X, sources[i] % GROUPS
        at = out.at[tile, pl.ds(pl.multiple_of(group * rows, rows), rows)]
        at = out if out.shape[0] == rows else at
        return pltpu.make_async_copy(made.at[i, j], at, stores.at[i, j])

    for i in range(count):
        fetch(i).start()
    block_rows = rows // ZQ
    rank = ranks // (Y * ZQ)
    for i in range(count):
        fetch(i).wait()
        shrink = lax.dot_general(
            held[i, :, :features],
            downs[...],
            (((1,), (1,)), ((), ())),
            preferred_element_type=jnp.float32,
        )
        block = lax.broadcasted_iota(jnp.int32, shrink.shape, 0) // block_rows
        adapter = lax.broadcasted_iota(jnp.int32, shrink.shape, 1) // rank
        low = jnp.where(block + sources[i] * ZQ == adapter, 0.5 * shrink, 0.0)
        held[i, :, features:] = low.astype(held.dtype)
        total = jnp.dot(held[i], table[...], preferred_element_type=jnp.float32)
        total = total.astype(made.dtype)
        for j, out in enumerate((keep, send)):
            made[i, j] = total[:, j * columns : (j + 1) * columns]
            store(i, j, out).start()
    for i in range(count):
        for j, out in enumerate((keep, send)):
            store(i, j, out).wait()


def partials(where, table, downs, offsets, chunks, keep=None):
    count, outs = len(chunks), [] if keep is None else [keep]
    rows, features = chunks[0].shape
    width, columns = table.shape[0], table.shape[1] // 2
    out = jax.ShapeDtypeStruct((X, GROUPS * rows, columns), table.dtype)
    last = jax.ShapeDtypeStruct((rows, columns), table.dtype)
    return pl.pallas_call(
        functools.partial(project, offsets),
        out_shape=(out, last if outs else out),
        in_specs=[SMEM, VMEM, VMEM] + [ANY] * (count + len(outs)),
        out_specs=(ANY, ANY),
        scratch_shapes=[
            pltpu.VMEM((count, rows, width), table.dtype),
            pltpu.VMEM((count, 2, rows, columns), table.dtype),
            pltpu.SemaphoreType.DMA((count,)),
            pltpu.SemaphoreType.DMA((count, 2)),
        ],
        input_output_aliases={3 + count: 0} if outs else {},
        compiler_params=PARAMS,
        cost_estimate=pl.CostEstimate(
            flops=4 * count * rows * width * columns,
            bytes_accessed=2 * count * rows * (features + 2 * columns) + 2 * table.size,
            transcendentals=0,
        ),
    )(where, table, downs, *chunks, *outs)


def local(
    tokens, query_key_value_weight, adapter_down_weight, adapter_up_weight, adapter_per_block
):
    y, p, q, x, zh, c = (lax.axis_index(a) for a in AXES)
    rows, features = tokens.shape
    columns = query_key_value_weight.shape[1]
    adapter, down, up = adapter_per_block, adapter_down_weight, adapter_up_weight
    where = jnp.stack([y, p, q, x, (c != p) * 1]).astype(jnp.int32)

    def over(axis, size, step):
        return lambda v: lax.ppermute(v, axis, [(i, (i + step) % size) for i in range(size)])

    def opposite(v):
        pairs = [(i, j) for i in range(Y) for j in range(C)]
        return lax.ppermute(
            v, ("y", "c"), [(i * C + j, (i + 1 - 2 * j) % Y * C + j) for i, j in pairs]
        )

    def step(operands, done=()):
        values = lax.optimization_barrier(tuple(v for _, v in operands) + tuple(done))
        return [f(v) for (f, _), v in zip(operands, values)]

    own = query_key_value_weight
    forward, back, to_p = over("y", Y, 1), over("y", Y, -1), over("p", ZP, 1)
    up_swapped = to_p(picked(where, adapter, up))
    chunk = joined(tokens, over("q", ZQ, 1)(tokens))
    swapped, up_1, down_1 = step([(to_p, own), (forward, chunk), (back, chunk)], [up_swapped])
    up_2, down_2 = step([(forward, up_1), (back, down_1)])
    up_3, down_3 = step([(forward, up_2), (back, down_2)])

    table, downs = placed(where, adapter, down, up, own, [swapped, up_swapped])
    up_3, down_3, table = lax.optimization_barrier((up_3, down_3, table))
    far_y = opposite(jnp.where(c == 0, up_3, down_3))
    chunks = [chunk, up_1, down_1, up_2, down_2, up_3, down_3]
    keep, send = partials(where, table, downs, OFFSETS[:-1], chunks)
    received = over("c", C, 1)(lax.optimization_barrier((send, far_y))[0])
    keep, last = partials(where, table, downs, OFFSETS[-1:], [far_y], keep)
    source = (y + Y // 2) % Y
    start = ((source // GROUPS - x + X) % X, source % GROUPS * ZQ * rows, 0)
    received = lax.dynamic_update_slice(received, over("c", C, 1)(last)[None], start)

    def added(d):
        return keep[d].astype(jnp.float32) + received[d].astype(jnp.float32)

    def moved(d):
        return over("x", X, d)(added(d).astype(jnp.bfloat16)).astype(jnp.float32)

    total = moved(1) + moved(3) + moved(2) + added(0)
    total = total.astype(jnp.bfloat16).reshape(ZH, ZQ * rows, columns)

    here = jnp.where(zh == 0, total[0], total[1])
    there = jnp.where(zh == 0, total[1], total[0])
    places = [(i, h, j) for i in range(ZP) for h in range(ZH) for j in range(C)]
    swap = [(i * 4 + h * 2 + j, j * 4 + h * 2 + i) for i, h, j in places]
    cross = [(i * 4 + h * 2 + j, j * 4 + (1 - h) * 2 + i) for i, h, j in places]
    far = lax.ppermute(there, ("p", "zh", "c"), cross)
    near = lax.ppermute(here, ("p", "zh", "c"), swap)
    out = near.astype(jnp.float32) + far.astype(jnp.float32)
    out = out.reshape(ZQ, rows, columns)
    out = jnp.where(q == 0, out, out[::-1])
    return out.reshape(ZQ * rows, columns).astype(jnp.bfloat16)


def solution(mesh):
    physical = Mesh(mesh.devices.reshape(Y, ZP, ZQ, X, ZH, C), AXES)
    return jax.shard_map(
        local,
        mesh=physical,
        in_specs=(
            P(DP, TENSOR),
            P(TENSOR, DP),
            P(None, None, TENSOR),
            P(None, None, DP),
            P(),
        ),
        out_specs=P(TENSOR, DP),
        check_vma=False,
    )
```

```python
import jax
import jax.numpy as jnp
from jax import lax
from jax.experimental import pallas as pl
from jax.experimental.pallas import tpu as pltpu
from jax.sharding import Mesh, PartitionSpec as P

Y, ZP, ZQ, X, ZH, C = 8, 2, 2, 4, 2, 2
AXES = ("y", "p", "q", "x", "zh", "c")
DP, TENSOR = ("y", "p", "q"), ("x", "zh", "c")
VMEM_BYTES = 48_000_000
SMALL_VMEM_BYTES = 16_000_000
DOWN_COLUMNS = 512


def flip(size):
    return [(i, i ^ 1) for i in range(size)]


def copied(moves):
    for move in moves:
        move.start()
    for move in moves:
        move.wait()


def join_features(first, second, out, sems):
    width = first.shape[1]
    copied(
        [
            pltpu.make_async_copy(v, out.at[:, pl.ds(i * width, width)], sems.at[i])
            for i, v in enumerate((first, second))
        ]
    )


def joined(first, second):
    rows, width = first.shape
    return pl.pallas_call(
        join_features,
        out_shape=jax.ShapeDtypeStruct((rows, 2 * width), first.dtype),
        in_specs=[pl.BlockSpec(memory_space=pltpu.VMEM)] * 2,
        out_specs=pl.BlockSpec(memory_space=pl.ANY),
        scratch_shapes=[pltpu.SemaphoreType.DMA((2,))],
        compiler_params=pltpu.CompilerParams(vmem_limit_bytes=SMALL_VMEM_BYTES),
    )(first, second)


def place_weights(slots, *refs):
    ins, (table, sems) = refs[:-2], refs[-2:]
    first, *halves = ins[:3]
    pair, *pair_halves = ins[3:6]
    up, up_swapped, down_own, down_pair = ins[6:]
    features, columns = first.shape
    moves = []

    def move(source, row, col):
        at = tuple(
            pl.ds(pl.multiple_of(i, 128), n) for i, n in zip((row, col), source.shape)
        )
        moves.append(pltpu.make_async_copy(source, table.at[at], sems.at[len(moves)]))

    own, other = slots[1] * columns, (1 - slots[1]) * columns
    for k, whole, split in ((slots[0], first, halves), (1 - slots[0], pair, pair_halves)):
        move(whole, k * features, own)
        for i, v in enumerate(split):
            move(v, k * features + i * v.shape[0], other)
    move(up, 2 * features, own)
    move(up_swapped, 2 * features, other)
    ranks = down_own.shape[0]
    for k, v in ((slots[0], down_own), (1 - slots[0], down_pair)):
        for i in range(features // DOWN_COLUMNS):
            row = 2 * features + ranks * (1 + k * (features // DOWN_COLUMNS) + i)
            move(v.at[:, pl.ds(i * DOWN_COLUMNS, DOWN_COLUMNS)], row, 0)
    copied(moves)


def placed(slots, parts):
    features, columns = parts[0].shape
    ranks = parts[-1].shape[0]
    down_rows = 2 * features // DOWN_COLUMNS * ranks
    return pl.pallas_call(
        place_weights,
        out_shape=pltpu.VMEM((2 * features + ranks + down_rows, 2 * columns), parts[0].dtype),
        in_specs=[pl.BlockSpec(memory_space=pltpu.SMEM)]
        + [pl.BlockSpec(memory_space=pl.ANY)] * len(parts),
        out_specs=pl.BlockSpec(memory_space=pltpu.VMEM),
        scratch_shapes=[pltpu.SemaphoreType.DMA((16,))],
        compiler_params=pltpu.CompilerParams(vmem_limit_bytes=SMALL_VMEM_BYTES),
    )(slots, *parts)


def project(order, tokens, table, keep, send, held, sems):
    step = pl.program_id(0)
    rows, features = tokens.shape[1:]
    ranks = held.shape[3] - features
    rank = ranks // Y
    tiles, tile_rows, columns = keep.shape
    groups = tile_rows // rows

    def fetch(t):
        at = pl.ds((t + order[0]) % X * groups, groups)
        return pltpu.make_async_copy(
            tokens.at[at], held.at[t, :, :, pl.ds(0, features)], sems.at[t]
        )

    @pl.when(step == 0)
    def _():
        for t in range(X):
            fetch(t).start()

    here = [step * tiles + i for i in range(tiles)]
    for t in here:
        fetch(t).wait()
    for t in here:
        shrink = 0.0
        for i in range(features // DOWN_COLUMNS):
            at = slice(i * DOWN_COLUMNS, (i + 1) * DOWN_COLUMNS)
            start = features + (1 + i) * ranks
            shrink += lax.dot_general(
                held[t, :, :, at].reshape(tile_rows, DOWN_COLUMNS),
                table[start : start + ranks, :DOWN_COLUMNS],
                (((1,), (1,)), ((), ())),
                preferred_element_type=jnp.float32,
            )
        block = lax.broadcasted_iota(jnp.int32, shrink.shape, 0) // rows
        block += (t + order[0]) % X * groups
        adapter = lax.broadcasted_iota(jnp.int32, shrink.shape, 1) // rank
        low = jnp.where(block == adapter, 0.5 * shrink, 0.0).astype(held.dtype)
        held[t, :, :, features:] = low.reshape(groups, rows, ranks)
    for i, t in enumerate(here):
        tok = held[t].reshape(tile_rows, features + ranks)
        total = jnp.dot(tok, table[: features + ranks], preferred_element_type=jnp.float32)
        total = total.astype(keep.dtype)
        keep[i] = total[:, :columns]
        send[i] = total[:, columns:]


def partials(x, gathered, table, ranks):
    rows, features = gathered.shape[1:]
    columns = table.shape[1] // 2
    groups = Y // X
    tiles = 2
    out = jax.ShapeDtypeStruct((X, groups * rows, columns), jnp.bfloat16)
    return pl.pallas_call(
        project,
        out_shape=(out, out),
        grid_spec=pltpu.PrefetchScalarGridSpec(
            num_scalar_prefetch=1,
            grid=(X // tiles,),
            in_specs=[
                pl.BlockSpec(memory_space=pltpu.HBM),
                pl.BlockSpec(memory_space=pltpu.VMEM),
            ],
            out_specs=[
                pl.BlockSpec((tiles,) + out.shape[1:], lambda t, order: (t, 0, 0))
            ]
            * 2,
            scratch_shapes=[
                pltpu.VMEM((X, groups, rows, features + ranks), jnp.bfloat16),
                pltpu.SemaphoreType.DMA((X,)),
            ],
        ),
        compiler_params=pltpu.CompilerParams(vmem_limit_bytes=VMEM_BYTES),
        cost_estimate=pl.CostEstimate(
            flops=4 * gathered.size * columns,
            bytes_accessed=2 * (gathered.size + table.size + 2 * out.size),
            transcendentals=0,
        ),
    )(x.reshape(1), gathered, table)


def local(
    tokens, query_key_value_weight, adapter_down_weight, adapter_up_weight, adapter_per_block
):
    p, q, x, zh, c = (lax.axis_index(a) for a in AXES[1:])
    rows, features = tokens.shape
    columns = query_key_value_weight.shape[1]
    half = x % 2
    order = jnp.where(q == half, 0, 1)

    grid = [(i, j) for i in range(ZQ) for j in range(X)]

    def over(target):
        return [(i * X + j, target(i, j)) for i, j in grid]

    first = lax.ppermute(
        tokens, ("q", "x"), over(lambda i, j: i * X + j if i == j % 2 else (1 - i) * X + (j ^ 1))
    )
    second = lax.ppermute(
        tokens, ("q", "x"), over(lambda i, j: (1 - i) * X + j if i == j % 2 else i * X + (j ^ 1))
    )
    gathered = lax.all_gather(joined(first, second), "y", axis=0, tiled=False)

    per = adapter_per_block.reshape(Y, ZP, ZQ)

    def adapters(i, j):
        return lax.dynamic_slice(per, (0, i, j), (Y, 1, 1)).reshape(Y)

    def taken(table, i, j):
        return table[adapters(i, j)].reshape(-1, table.shape[2])

    down = taken(adapter_down_weight, p, half)
    down_pair = lax.ppermute(taken(adapter_down_weight, p, 1 - half), "x", flip(X))
    up = taken(adapter_up_weight, p, half)
    up_swapped = lax.ppermute(taken(adapter_up_weight, 1 - p, half), "p", flip(ZP))

    own = query_key_value_weight
    pair = lax.ppermute(own, "x", flip(X))
    swapped = [lax.ppermute(v, "p", flip(ZP)) for v in jnp.split(own, 2)]
    swapped_pair = [lax.ppermute(v, "x", flip(X)) for v in swapped]
    slots = jnp.stack([order, jnp.where(c == p, 0, 1)]).astype(jnp.int32)
    table = placed(
        slots, [own, *swapped, pair, *swapped_pair, up, up_swapped, down, down_pair]
    )

    keep, send = partials(x, gathered, table, down.shape[0])
    received = lax.ppermute(send, "c", flip(C))

    def added(d):
        return keep[d].astype(jnp.float32) + received[d].astype(jnp.float32)

    def moved(d):
        shift = [(i, (i + d) % X) for i in range(X)]
        return lax.ppermute(added(d).astype(jnp.bfloat16), "x", shift).astype(jnp.float32)

    places = [(i, h, j) for i in range(ZP) for h in range(ZH) for j in range(C)]
    swap = [(i * 4 + h * 2 + j, j * 4 + h * 2 + i) for i, h, j in places]
    cross = [(i * 4 + h * 2 + j, j * 4 + (1 - h) * 2 + i) for i, h, j in places]

    def split(total):
        total = total.astype(jnp.bfloat16).reshape(ZH, rows, columns)
        here = jnp.where(zh == 0, total[0], total[1])
        there = jnp.where(zh == 0, total[1], total[0])
        return here, there

    def sent(value, pairs):
        return lax.ppermute(value, ("p", "zh", "c"), pairs)

    from_2, from_3, from_1 = moved(2), moved(3), moved(1)
    here, there = split(added(0) + from_2)
    far = sent(there, cross)
    near = sent(here, swap)
    here, there = split(from_3 + from_1)
    far_beside = sent(there, cross)
    near_beside = sent(here, swap)
    out = jnp.stack([near, near_beside]).astype(jnp.float32)
    out += jnp.stack([far, far_beside]).astype(jnp.float32)
    out = jnp.where(half == 0, out, out[::-1])
    return out.reshape(ZQ * rows, columns).astype(jnp.bfloat16)


def solution(mesh):
    physical = Mesh(mesh.devices.reshape(Y, ZP, ZQ, X, ZH, C), AXES)
    return jax.shard_map(
        local,
        mesh=physical,
        in_specs=(
            P(DP, TENSOR),
            P(TENSOR, DP),
            P(None, None, TENSOR),
            P(None, None, DP),
            P(),
        ),
        out_specs=P(TENSOR, DP),
        check_vma=False,
    )
```

```python
import jax
import jax.numpy as jnp
from jax import lax
from jax.experimental import pallas as pl
from jax.experimental.pallas import tpu as pltpu
from jax.sharding import Mesh, PartitionSpec as P

Y, ZP, ZQ, X, ZH, C = 8, 2, 2, 4, 2, 2
AXES = ("y", "p", "q", "x", "zh", "c")
DP, TENSOR = ("y", "p", "q"), ("x", "zh", "c")
VMEM_BYTES = 48_000_000
SMALL_VMEM_BYTES = 16_000_000
DOWN_COLUMNS = 512


def flip(size):
    return [(i, i ^ 1) for i in range(size)]


def copied(moves):
    for move in moves:
        move.start()
    for move in moves:
        move.wait()


def join_features(first, second, out, sems):
    width = first.shape[1]
    copied(
        [
            pltpu.make_async_copy(v, out.at[:, pl.ds(i * width, width)], sems.at[i])
            for i, v in enumerate((first, second))
        ]
    )


def joined(first, second):
    rows, width = first.shape
    return pl.pallas_call(
        join_features,
        out_shape=jax.ShapeDtypeStruct((rows, 2 * width), first.dtype),
        in_specs=[pl.BlockSpec(memory_space=pltpu.VMEM)] * 2,
        out_specs=pl.BlockSpec(memory_space=pl.ANY),
        scratch_shapes=[pltpu.SemaphoreType.DMA((2,))],
        compiler_params=pltpu.CompilerParams(vmem_limit_bytes=SMALL_VMEM_BYTES),
    )(first, second)


def place_weights(slots, *refs):
    ins, (table, sems) = refs[:-2], refs[-2:]
    first, *halves = ins[:3]
    pair, *pair_halves = ins[3:6]
    up, up_swapped, down_own, down_pair = ins[6:]
    features, columns = first.shape
    moves = []

    def move(source, row, col):
        at = tuple(
            pl.ds(pl.multiple_of(i, 128), n) for i, n in zip((row, col), source.shape)
        )
        moves.append(pltpu.make_async_copy(source, table.at[at], sems.at[len(moves)]))

    own, other = slots[1] * columns, (1 - slots[1]) * columns
    for k, whole, split in ((slots[0], first, halves), (1 - slots[0], pair, pair_halves)):
        move(whole, k * features, own)
        for i, v in enumerate(split):
            move(v, k * features + i * v.shape[0], other)
    move(up, 2 * features, own)
    move(up_swapped, 2 * features, other)
    ranks = down_own.shape[0]
    for k, v in ((slots[0], down_own), (1 - slots[0], down_pair)):
        for i in range(features // DOWN_COLUMNS):
            row = 2 * features + ranks * (1 + k * (features // DOWN_COLUMNS) + i)
            move(v.at[:, pl.ds(i * DOWN_COLUMNS, DOWN_COLUMNS)], row, 0)
    copied(moves)


def placed(slots, parts):
    features, columns = parts[0].shape
    ranks = parts[-1].shape[0]
    down_rows = 2 * features // DOWN_COLUMNS * ranks
    return pl.pallas_call(
        place_weights,
        out_shape=pltpu.VMEM((2 * features + ranks + down_rows, 2 * columns), parts[0].dtype),
        in_specs=[pl.BlockSpec(memory_space=pltpu.SMEM)]
        + [pl.BlockSpec(memory_space=pl.ANY)] * len(parts),
        out_specs=pl.BlockSpec(memory_space=pltpu.VMEM),
        scratch_shapes=[pltpu.SemaphoreType.DMA((16,))],
        compiler_params=pltpu.CompilerParams(vmem_limit_bytes=SMALL_VMEM_BYTES),
    )(slots, *parts)


def project(order, tokens, table, keep, send, held, sems):
    step = pl.program_id(0)
    rows, features = tokens.shape[1:]
    ranks = held.shape[3] - features
    rank = ranks // Y
    tiles, tile_rows, columns = keep.shape
    groups = tile_rows // rows

    def fetch(t):
        at = pl.ds((t + order[0]) % X * groups, groups)
        return pltpu.make_async_copy(
            tokens.at[at], held.at[t, :, :, pl.ds(0, features)], sems.at[t]
        )

    @pl.when(step == 0)
    def _():
        for t in range(X):
            fetch(t).start()

    here = [step * tiles + i for i in range(tiles)]
    for t in here:
        fetch(t).wait()
    for t in here:
        shrink = 0.0
        for i in range(features // DOWN_COLUMNS):
            at = slice(i * DOWN_COLUMNS, (i + 1) * DOWN_COLUMNS)
            start = features + (1 + i) * ranks
            shrink += lax.dot_general(
                held[t, :, :, at].reshape(tile_rows, DOWN_COLUMNS),
                table[start : start + ranks, :DOWN_COLUMNS],
                (((1,), (1,)), ((), ())),
                preferred_element_type=jnp.float32,
            )
        block = lax.broadcasted_iota(jnp.int32, shrink.shape, 0) // rows
        block += (t + order[0]) % X * groups
        adapter = lax.broadcasted_iota(jnp.int32, shrink.shape, 1) // rank
        low = jnp.where(block == adapter, 0.5 * shrink, 0.0).astype(held.dtype)
        held[t, :, :, features:] = low.reshape(groups, rows, ranks)
    for i, t in enumerate(here):
        tok = held[t].reshape(tile_rows, features + ranks)
        total = jnp.dot(tok, table[: features + ranks], preferred_element_type=jnp.float32)
        total = total.astype(keep.dtype)
        keep[i] = total[:, :columns]
        send[i] = total[:, columns:]


def partials(x, gathered, table, ranks):
    rows, features = gathered.shape[1:]
    columns = table.shape[1] // 2
    groups = Y // X
    tiles = 2
    out = jax.ShapeDtypeStruct((X, groups * rows, columns), jnp.bfloat16)
    return pl.pallas_call(
        project,
        out_shape=(out, out),
        grid_spec=pltpu.PrefetchScalarGridSpec(
            num_scalar_prefetch=1,
            grid=(X // tiles,),
            in_specs=[
                pl.BlockSpec(memory_space=pltpu.HBM),
                pl.BlockSpec(memory_space=pltpu.VMEM),
            ],
            out_specs=[
                pl.BlockSpec((tiles,) + out.shape[1:], lambda t, order: (t, 0, 0))
            ]
            * 2,
            scratch_shapes=[
                pltpu.VMEM((X, groups, rows, features + ranks), jnp.bfloat16),
                pltpu.SemaphoreType.DMA((X,)),
            ],
        ),
        compiler_params=pltpu.CompilerParams(vmem_limit_bytes=VMEM_BYTES),
        cost_estimate=pl.CostEstimate(
            flops=4 * gathered.size * columns,
            bytes_accessed=2 * (gathered.size + table.size + 2 * out.size),
            transcendentals=0,
        ),
    )(x.reshape(1), gathered, table)


def local(
    tokens, query_key_value_weight, adapter_down_weight, adapter_up_weight, adapter_per_block
):
    p, q, x, zh, c = (lax.axis_index(a) for a in AXES[1:])
    rows, features = tokens.shape
    columns = query_key_value_weight.shape[1]
    half = x % 2
    order = jnp.where(q == half, 0, 1)

    grid = [(i, j) for i in range(ZQ) for j in range(X)]

    def over(target):
        return [(i * X + j, target(i, j)) for i, j in grid]

    first = lax.ppermute(
        tokens, ("q", "x"), over(lambda i, j: i * X + j if i == j % 2 else (1 - i) * X + (j ^ 1))
    )
    second = lax.ppermute(
        tokens, ("q", "x"), over(lambda i, j: (1 - i) * X + j if i == j % 2 else i * X + (j ^ 1))
    )
    gathered = lax.all_gather(joined(first, second), "y", axis=0, tiled=False)

    per = adapter_per_block.reshape(Y, ZP, ZQ)

    def adapters(i, j):
        return lax.dynamic_slice(per, (0, i, j), (Y, 1, 1)).reshape(Y)

    def taken(table, i, j):
        return table[adapters(i, j)].reshape(-1, table.shape[2])

    down = taken(adapter_down_weight, p, half)
    down_pair = lax.ppermute(taken(adapter_down_weight, p, 1 - half), "x", flip(X))
    up = taken(adapter_up_weight, p, half)
    up_swapped = lax.ppermute(taken(adapter_up_weight, 1 - p, half), "p", flip(ZP))

    own = query_key_value_weight
    pair = lax.ppermute(own, "x", flip(X))
    swapped = [lax.ppermute(v, "p", flip(ZP)) for v in jnp.split(own, 2)]
    swapped_pair = [lax.ppermute(v, "x", flip(X)) for v in swapped]
    slots = jnp.stack([order, jnp.where(c == p, 0, 1)]).astype(jnp.int32)
    table = placed(
        slots, [own, *swapped, pair, *swapped_pair, up, up_swapped, down, down_pair]
    )

    keep, send = partials(x, gathered, table, down.shape[0])
    received = lax.ppermute(send, "c", flip(C))

    def added(d):
        return keep[d].astype(jnp.float32) + received[d].astype(jnp.float32)

    def moved(d):
        shift = [(i, (i + d) % X) for i in range(X)]
        return lax.ppermute(added(d).astype(jnp.bfloat16), "x", shift).astype(jnp.float32)

    places = [(i, h, j) for i in range(ZP) for h in range(ZH) for j in range(C)]
    swap = [(i * 4 + h * 2 + j, j * 4 + h * 2 + i) for i, h, j in places]
    cross = [(i * 4 + h * 2 + j, j * 4 + (1 - h) * 2 + i) for i, h, j in places]

    def split(total):
        total = total.astype(jnp.bfloat16).reshape(ZH, rows, columns)
        here = jnp.where(zh == 0, total[0], total[1])
        there = jnp.where(zh == 0, total[1], total[0])
        return here, there

    def sent(value, pairs):
        return lax.ppermute(value, ("p", "zh", "c"), pairs)

    from_2, from_3, from_1 = moved(2), moved(3), moved(1)
    here, there = split(added(0) + from_2)
    far = sent(there, cross)
    near = sent(here, swap)
    here, there = split(from_3 + from_1)
    far_beside = sent(there, cross)
    near_beside = sent(here, swap)
    out = jnp.stack([far, far_beside]).astype(jnp.float32)
    out += jnp.stack([near, near_beside]).astype(jnp.float32)
    out = jnp.where(half == 0, out, out[::-1])
    return out.reshape(ZQ * rows, columns).astype(jnp.bfloat16)


def solution(mesh):
    physical = Mesh(mesh.devices.reshape(Y, ZP, ZQ, X, ZH, C), AXES)
    return jax.shard_map(
        local,
        mesh=physical,
        in_specs=(
            P(DP, TENSOR),
            P(TENSOR, DP),
            P(None, None, TENSOR),
            P(None, None, DP),
            P(),
        ),
        out_specs=P(TENSOR, DP),
        check_vma=False,
    )
```

```python
import functools

import jax
import jax.numpy as jnp
from jax import lax
from jax.experimental import pallas as pl
from jax.experimental.pallas import tpu as pltpu
from jax.sharding import Mesh, PartitionSpec as P

Y, ZP, ZQ, X, ZH, C = 8, 2, 2, 4, 2, 2
AXES = ("y", "p", "q", "x", "zh", "c")
DP, TENSOR = ("y", "p", "q"), ("x", "zh", "c")
VMEM_BYTES = 48_000_000
SMALL_VMEM_BYTES = 16_000_000
DOWN_COLUMNS = 512


def flip(size):
    return [(i, i ^ 1) for i in range(size)]


def copied(moves):
    for move in moves:
        move.start()
    for move in moves:
        move.wait()


def join_features(first, second, out, sems):
    width = first.shape[1]
    copied(
        [
            pltpu.make_async_copy(v, out.at[:, pl.ds(i * width, width)], sems.at[i])
            for i, v in enumerate((first, second))
        ]
    )


def joined(first, second):
    rows, width = first.shape
    return pl.pallas_call(
        join_features,
        out_shape=jax.ShapeDtypeStruct((rows, 2 * width), first.dtype),
        in_specs=[pl.BlockSpec(memory_space=pltpu.VMEM)] * 2,
        out_specs=pl.BlockSpec(memory_space=pl.ANY),
        scratch_shapes=[pltpu.SemaphoreType.DMA((2,))],
        compiler_params=pltpu.CompilerParams(vmem_limit_bytes=SMALL_VMEM_BYTES),
    )(first, second)


def place_weights(slots, *refs):
    ins, (table, sems) = refs[:-2], refs[-2:]
    first, *halves = ins[:3]
    pair, *pair_halves = ins[3:6]
    up, up_swapped, down_own, down_pair = ins[6:]
    features, columns = first.shape
    moves = []

    def move(source, row, col):
        at = tuple(
            pl.ds(pl.multiple_of(i, 128), n) for i, n in zip((row, col), source.shape)
        )
        moves.append(pltpu.make_async_copy(source, table.at[at], sems.at[len(moves)]))

    own, other = slots[1] * columns, (1 - slots[1]) * columns
    for k, whole, split in ((slots[0], first, halves), (1 - slots[0], pair, pair_halves)):
        move(whole, k * features, own)
        for i, v in enumerate(split):
            move(v, k * features + i * v.shape[0], other)
    move(up, 2 * features, own)
    move(up_swapped, 2 * features, other)
    ranks = down_own.shape[0]
    for k, v in ((slots[0], down_own), (1 - slots[0], down_pair)):
        for i in range(features // DOWN_COLUMNS):
            row = 2 * features + ranks * (1 + k * (features // DOWN_COLUMNS) + i)
            move(v.at[:, pl.ds(i * DOWN_COLUMNS, DOWN_COLUMNS)], row, 0)
    copied(moves)


def placed(slots, parts):
    features, columns = parts[0].shape
    ranks = parts[-1].shape[0]
    down_rows = 2 * features // DOWN_COLUMNS * ranks
    return pl.pallas_call(
        place_weights,
        out_shape=pltpu.VMEM((2 * features + ranks + down_rows, 2 * columns), parts[0].dtype),
        in_specs=[pl.BlockSpec(memory_space=pltpu.SMEM)]
        + [pl.BlockSpec(memory_space=pl.ANY)] * len(parts),
        out_specs=pl.BlockSpec(memory_space=pltpu.VMEM),
        scratch_shapes=[pltpu.SemaphoreType.DMA((16,))],
        compiler_params=pltpu.CompilerParams(vmem_limit_bytes=SMALL_VMEM_BYTES),
    )(slots, *parts)


def project(base, order, tokens, table, keep, send, held, sems):
    rows, features = tokens.shape[1:]
    ranks = held.shape[3] - features
    rank = ranks // Y
    tiles, tile_rows, columns = keep.shape
    groups = tile_rows // rows

    def fetch(t):
        at = pl.ds((base + t + order[0]) % X * groups, groups)
        return pltpu.make_async_copy(
            tokens.at[at], held.at[t, :, :, pl.ds(0, features)], sems.at[t]
        )

    here = range(tiles)
    for t in here:
        fetch(t).start()
    for t in here:
        fetch(t).wait()
    for t in here:
        shrink = 0.0
        for i in range(features // DOWN_COLUMNS):
            at = slice(i * DOWN_COLUMNS, (i + 1) * DOWN_COLUMNS)
            start = features + (1 + i) * ranks
            shrink += lax.dot_general(
                held[t, :, :, at].reshape(tile_rows, DOWN_COLUMNS),
                table[start : start + ranks, :DOWN_COLUMNS],
                (((1,), (1,)), ((), ())),
                preferred_element_type=jnp.float32,
            )
        block = lax.broadcasted_iota(jnp.int32, shrink.shape, 0) // rows
        block += (base + t + order[0]) % X * groups
        adapter = lax.broadcasted_iota(jnp.int32, shrink.shape, 1) // rank
        low = jnp.where(block == adapter, 0.5 * shrink, 0.0).astype(held.dtype)
        held[t, :, :, features:] = low.reshape(groups, rows, ranks)
    for i, t in enumerate(here):
        tok = held[t].reshape(tile_rows, features + ranks)
        total = jnp.dot(tok, table[: features + ranks], preferred_element_type=jnp.float32)
        total = total.astype(keep.dtype)
        keep[i] = total[:, :columns]
        send[i] = total[:, columns:]


def partials(x, gathered, table, ranks, base):
    rows, features = gathered.shape[1:]
    columns = table.shape[1] // 2
    groups = Y // X
    tiles = 2
    out = jax.ShapeDtypeStruct((tiles, groups * rows, columns), jnp.bfloat16)
    return pl.pallas_call(
        functools.partial(project, base),
        out_shape=(out, out),
        grid_spec=pltpu.PrefetchScalarGridSpec(
            num_scalar_prefetch=1,
            grid=(1,),
            in_specs=[
                pl.BlockSpec(memory_space=pltpu.HBM),
                pl.BlockSpec(memory_space=pltpu.VMEM),
            ],
            out_specs=[
                pl.BlockSpec((tiles,) + out.shape[1:], lambda t, order: (t, 0, 0))
            ]
            * 2,
            scratch_shapes=[
                pltpu.VMEM((tiles, groups, rows, features + ranks), jnp.bfloat16),
                pltpu.SemaphoreType.DMA((tiles,)),
            ],
        ),
        compiler_params=pltpu.CompilerParams(vmem_limit_bytes=VMEM_BYTES),
        cost_estimate=pl.CostEstimate(
            flops=2 * gathered.size * columns,
            bytes_accessed=2 * (gathered.size // 2 + table.size + 2 * out.size),
            transcendentals=0,
        ),
    )(x.reshape(1), gathered, table)


def local(
    tokens, query_key_value_weight, adapter_down_weight, adapter_up_weight, adapter_per_block
):
    p, q, x, zh, c = (lax.axis_index(a) for a in AXES[1:])
    rows, features = tokens.shape
    columns = query_key_value_weight.shape[1]
    half = x % 2
    order = jnp.where(q == half, 0, 1)

    grid = [(i, j) for i in range(ZQ) for j in range(X)]

    def over(target):
        return [(i * X + j, target(i, j)) for i, j in grid]

    first = lax.ppermute(
        tokens, ("q", "x"), over(lambda i, j: i * X + j if i == j % 2 else (1 - i) * X + (j ^ 1))
    )
    second = lax.ppermute(
        tokens, ("q", "x"), over(lambda i, j: (1 - i) * X + j if i == j % 2 else i * X + (j ^ 1))
    )
    gathered = lax.all_gather(joined(first, second), "y", axis=0, tiled=False)

    per = adapter_per_block.reshape(Y, ZP, ZQ)

    def adapters(i, j):
        return lax.dynamic_slice(per, (0, i, j), (Y, 1, 1)).reshape(Y)

    def taken(table, i, j):
        return table[adapters(i, j)].reshape(-1, table.shape[2])

    down = taken(adapter_down_weight, p, half)
    down_pair = lax.ppermute(taken(adapter_down_weight, p, 1 - half), "x", flip(X))
    up = taken(adapter_up_weight, p, half)
    up_swapped = lax.ppermute(taken(adapter_up_weight, 1 - p, half), "p", flip(ZP))

    own = query_key_value_weight
    pair = lax.ppermute(own, "x", flip(X))
    swapped = [lax.ppermute(v, "p", flip(ZP)) for v in jnp.split(own, 2)]
    swapped_pair = [lax.ppermute(v, "x", flip(X)) for v in swapped]
    slots = jnp.stack([order, jnp.where(c == p, 0, 1)]).astype(jnp.int32)
    table = placed(
        slots, [own, *swapped, pair, *swapped_pair, up, up_swapped, down, down_pair]
    )

    keep, received = {}, {}
    for base in (2, 0):
        kept, send = partials(x, gathered, table, down.shape[0], base)
        got = lax.ppermute(send, "c", flip(C))
        for i in range(2):
            keep[base + i], received[base + i] = kept[i], got[i]

    def added(d):
        return keep[d].astype(jnp.float32) + received[d].astype(jnp.float32)

    def moved(d):
        shift = [(i, (i + d) % X) for i in range(X)]
        return lax.ppermute(added(d).astype(jnp.bfloat16), "x", shift).astype(jnp.float32)

    places = [(i, h, j) for i in range(ZP) for h in range(ZH) for j in range(C)]
    swap = [(i * 4 + h * 2 + j, j * 4 + h * 2 + i) for i, h, j in places]
    cross = [(i * 4 + h * 2 + j, j * 4 + (1 - h) * 2 + i) for i, h, j in places]

    def split(total):
        total = total.astype(jnp.bfloat16).reshape(ZH, rows, columns)
        here = jnp.where(zh == 0, total[0], total[1])
        there = jnp.where(zh == 0, total[1], total[0])
        return here, there

    def sent(value, pairs):
        return lax.ppermute(value, ("p", "zh", "c"), pairs)

    from_2, from_3, from_1 = moved(2), moved(3), moved(1)
    here, there = split(added(0) + from_2)
    far = sent(there, cross)
    near = sent(here, swap)
    here, there = split(from_3 + from_1)
    far_beside = sent(there, cross)
    near_beside = sent(here, swap)
    out = jnp.stack([far, far_beside]).astype(jnp.float32)
    out += jnp.stack([near, near_beside]).astype(jnp.float32)
    out = jnp.where(half == 0, out, out[::-1])
    return out.reshape(ZQ * rows, columns).astype(jnp.bfloat16)


def solution(mesh):
    physical = Mesh(mesh.devices.reshape(Y, ZP, ZQ, X, ZH, C), AXES)
    return jax.shard_map(
        local,
        mesh=physical,
        in_specs=(
            P(DP, TENSOR),
            P(TENSOR, DP),
            P(None, None, TENSOR),
            P(None, None, DP),
            P(),
        ),
        out_specs=P(TENSOR, DP),
        check_vma=False,
    )
```

```python
import jax
import jax.numpy as jnp
from jax import lax
from jax.experimental import pallas as pl
from jax.experimental.pallas import tpu as pltpu
from jax.sharding import Mesh, PartitionSpec as P

Y, ZP, ZQ, X, ZH, C = 8, 2, 2, 4, 2, 2
AXES = ("y", "p", "q", "x", "zh", "c")
DP, TENSOR = ("y", "p", "q"), ("x", "zh", "c")
VMEM_BYTES = 48_000_000
SMALL_VMEM_BYTES = 16_000_000
DOWN_COLUMNS = 768


def flip(size):
    return [(i, i ^ 1) for i in range(size)]


def copied(moves):
    for move in moves:
        move.start()
    for move in moves:
        move.wait()


def join_features(first, second, out, sems):
    width = first.shape[1]
    copied(
        [
            pltpu.make_async_copy(v, out.at[:, pl.ds(i * width, width)], sems.at[i])
            for i, v in enumerate((first, second))
        ]
    )


def joined(first, second):
    rows, width = first.shape
    return pl.pallas_call(
        join_features,
        out_shape=jax.ShapeDtypeStruct((rows, 2 * width), first.dtype),
        in_specs=[pl.BlockSpec(memory_space=pltpu.VMEM)] * 2,
        out_specs=pl.BlockSpec(memory_space=pl.ANY),
        scratch_shapes=[pltpu.SemaphoreType.DMA((2,))],
        compiler_params=pltpu.CompilerParams(vmem_limit_bytes=SMALL_VMEM_BYTES),
    )(first, second)


def place_weights(slots, *refs):
    ins, (table, sems) = refs[:-2], refs[-2:]
    first, *halves = ins[:3]
    pair, *pair_halves = ins[3:6]
    up, up_swapped, down_own, down_pair = ins[6:]
    features, columns = first.shape
    moves = []

    def move(source, row, col):
        at = tuple(
            pl.ds(pl.multiple_of(i, 128), n) for i, n in zip((row, col), source.shape)
        )
        moves.append(pltpu.make_async_copy(source, table.at[at], sems.at[len(moves)]))

    own, other = slots[1] * columns, (1 - slots[1]) * columns
    for k, whole, split in ((slots[0], first, halves), (1 - slots[0], pair, pair_halves)):
        move(whole, k * features, own)
        for i, v in enumerate(split):
            move(v, k * features + i * v.shape[0], other)
    move(up, 2 * features, own)
    move(up_swapped, 2 * features, other)
    ranks = down_own.shape[0]
    for k, v in ((slots[0], down_own), (1 - slots[0], down_pair)):
        rest = features - DOWN_COLUMNS
        move(v.at[:, pl.ds(0, DOWN_COLUMNS)], 2 * features + ranks * (1 + k), 0)
        move(v.at[:, pl.ds(DOWN_COLUMNS, rest)], 2 * features + ranks * 3, k * rest)
    copied(moves)


def placed(slots, parts):
    features, columns = parts[0].shape
    ranks = parts[-1].shape[0]
    down_rows = 3 * ranks
    return pl.pallas_call(
        place_weights,
        out_shape=pltpu.VMEM((2 * features + ranks + down_rows, 2 * columns), parts[0].dtype),
        in_specs=[pl.BlockSpec(memory_space=pltpu.SMEM)]
        + [pl.BlockSpec(memory_space=pl.ANY)] * len(parts),
        out_specs=pl.BlockSpec(memory_space=pltpu.VMEM),
        scratch_shapes=[pltpu.SemaphoreType.DMA((16,))],
        compiler_params=pltpu.CompilerParams(vmem_limit_bytes=SMALL_VMEM_BYTES),
    )(slots, *parts)


def project(order, tokens, table, keep, send, held, sems):
    step = pl.program_id(0)
    rows, features = tokens.shape[1:]
    ranks = held.shape[3] - features
    rank = ranks // Y
    tiles, tile_rows, columns = keep.shape
    groups = tile_rows // rows

    def fetch(t):
        at = pl.ds((t + order[0]) % X * groups, groups)
        return pltpu.make_async_copy(
            tokens.at[at], held.at[t, :, :, pl.ds(0, features)], sems.at[t]
        )

    @pl.when(step == 0)
    def _():
        for t in range(X):
            fetch(t).start()

    here = [step * tiles + i for i in range(tiles)]
    for t in here:
        fetch(t).wait()
    for t in here:
        shrink = 0.0
        part = features // 2
        rest = part - DOWN_COLUMNS
        for k in range(2):
            for row, col, begin, count in (
                (1 + k, 0, k * part, DOWN_COLUMNS),
                (3, k * rest, k * part + DOWN_COLUMNS, rest),
            ):
                start = features + row * ranks
                shrink += lax.dot_general(
                    held[t, :, :, begin : begin + count].reshape(tile_rows, count),
                    table[start : start + ranks, col : col + count],
                    (((1,), (1,)), ((), ())),
                    preferred_element_type=jnp.float32,
                )
        block = lax.broadcasted_iota(jnp.int32, shrink.shape, 0) // rows
        block += (t + order[0]) % X * groups
        adapter = lax.broadcasted_iota(jnp.int32, shrink.shape, 1) // rank
        low = jnp.where(block == adapter, 0.5 * shrink, 0.0).astype(held.dtype)
        held[t, :, :, features:] = low.reshape(groups, rows, ranks)
    for i, t in enumerate(here):
        tok = held[t].reshape(tile_rows, features + ranks)
        total = jnp.dot(tok, table[: features + ranks], preferred_element_type=jnp.float32)
        total = total.astype(keep.dtype)
        keep[i] = total[:, :columns]
        send[i] = total[:, columns:]


def partials(x, gathered, table, ranks):
    rows, features = gathered.shape[1:]
    columns = table.shape[1] // 2
    groups = Y // X
    tiles = 2
    out = jax.ShapeDtypeStruct((X, groups * rows, columns), jnp.bfloat16)
    return pl.pallas_call(
        project,
        out_shape=(out, out),
        grid_spec=pltpu.PrefetchScalarGridSpec(
            num_scalar_prefetch=1,
            grid=(X // tiles,),
            in_specs=[
                pl.BlockSpec(memory_space=pltpu.HBM),
                pl.BlockSpec(memory_space=pltpu.VMEM),
            ],
            out_specs=[
                pl.BlockSpec((tiles,) + out.shape[1:], lambda t, order: (t, 0, 0))
            ]
            * 2,
            scratch_shapes=[
                pltpu.VMEM((X, groups, rows, features + ranks), jnp.bfloat16),
                pltpu.SemaphoreType.DMA((X,)),
            ],
        ),
        compiler_params=pltpu.CompilerParams(vmem_limit_bytes=VMEM_BYTES),
        cost_estimate=pl.CostEstimate(
            flops=4 * gathered.size * columns,
            bytes_accessed=2 * (gathered.size + table.size + 2 * out.size),
            transcendentals=0,
        ),
    )(x.reshape(1), gathered, table)


def local(
    tokens, query_key_value_weight, adapter_down_weight, adapter_up_weight, adapter_per_block
):
    p, q, x, zh, c = (lax.axis_index(a) for a in AXES[1:])
    rows, features = tokens.shape
    columns = query_key_value_weight.shape[1]
    half = x % 2
    order = jnp.where(q == half, 0, 1)

    grid = [(i, j) for i in range(ZQ) for j in range(X)]

    def over(target):
        return [(i * X + j, target(i, j)) for i, j in grid]

    first = lax.ppermute(
        tokens, ("q", "x"), over(lambda i, j: i * X + j if i == j % 2 else (1 - i) * X + (j ^ 1))
    )
    second = lax.ppermute(
        tokens, ("q", "x"), over(lambda i, j: (1 - i) * X + j if i == j % 2 else i * X + (j ^ 1))
    )
    gathered = lax.all_gather(joined(first, second), "y", axis=0, tiled=False)

    per = adapter_per_block.reshape(Y, ZP, ZQ)

    def adapters(i, j):
        return lax.dynamic_slice(per, (0, i, j), (Y, 1, 1)).reshape(Y)

    def taken(table, i, j):
        return table[adapters(i, j)].reshape(-1, table.shape[2])

    down = taken(adapter_down_weight, p, half)
    down_pair = lax.ppermute(taken(adapter_down_weight, p, 1 - half), "x", flip(X))
    up = taken(adapter_up_weight, p, half)
    up_swapped = lax.ppermute(taken(adapter_up_weight, 1 - p, half), "p", flip(ZP))

    own = query_key_value_weight
    pair = lax.ppermute(own, "x", flip(X))
    swapped = [lax.ppermute(v, "p", flip(ZP)) for v in jnp.split(own, 2)]
    swapped_pair = [lax.ppermute(v, "x", flip(X)) for v in swapped]
    slots = jnp.stack([order, jnp.where(c == p, 0, 1)]).astype(jnp.int32)
    table = placed(
        slots, [own, *swapped, pair, *swapped_pair, up, up_swapped, down, down_pair]
    )

    keep, send = partials(x, gathered, table, down.shape[0])
    received = lax.ppermute(send, "c", flip(C))

    def added(d):
        return keep[d].astype(jnp.float32) + received[d].astype(jnp.float32)

    def moved(d):
        shift = [(i, (i + d) % X) for i in range(X)]
        return lax.ppermute(added(d).astype(jnp.bfloat16), "x", shift).astype(jnp.float32)

    places = [(i, h, j) for i in range(ZP) for h in range(ZH) for j in range(C)]
    swap = [(i * 4 + h * 2 + j, j * 4 + h * 2 + i) for i, h, j in places]
    cross = [(i * 4 + h * 2 + j, j * 4 + (1 - h) * 2 + i) for i, h, j in places]

    def split(total):
        total = total.astype(jnp.bfloat16).reshape(ZH, rows, columns)
        here = jnp.where(zh == 0, total[0], total[1])
        there = jnp.where(zh == 0, total[1], total[0])
        return here, there

    def sent(value, pairs):
        return lax.ppermute(value, ("p", "zh", "c"), pairs)

    from_2, from_3, from_1 = moved(2), moved(3), moved(1)
    here, there = split(added(0) + from_2)
    far = sent(there, cross)
    near = sent(here, swap)
    here, there = split(from_3 + from_1)
    far_beside = sent(there, cross)
    near_beside = sent(here, swap)
    out = jnp.stack([far, far_beside]).astype(jnp.float32)
    out += jnp.stack([near, near_beside]).astype(jnp.float32)
    out = jnp.where(half == 0, out, out[::-1])
    return out.reshape(ZQ * rows, columns).astype(jnp.bfloat16)


def solution(mesh):
    physical = Mesh(mesh.devices.reshape(Y, ZP, ZQ, X, ZH, C), AXES)
    return jax.shard_map(
        local,
        mesh=physical,
        in_specs=(
            P(DP, TENSOR),
            P(TENSOR, DP),
            P(None, None, TENSOR),
            P(None, None, DP),
            P(),
        ),
        out_specs=P(TENSOR, DP),
        check_vma=False,
    )
```
